512 devices in a mesh: rep: 4 (over y), ctx: 16 (over x, z_hi, core), tp: 8 (over z_lo).
Axes of the slice: x: 4, y: 4, z: 16 (z_hi: 2, z_lo: 8; z = z_hi * 8 + z_lo), core: 2. Of those that a mesh axis runs over, the one named last changes fastest.
Arguments:
- queries: bfloat16 [8, 512, 8192], P('rep', 'ctx', 'tp'), parts along dimension 0, may hold values from -200 to 200
- cache_keys: bfloat16 [8, 16384, 1024], P('rep', 'ctx', 'tp'), parts along dimension 0, may hold values from -8.1 to 8.1
- stored_values: bfloat16 [8, 16384, 1024], P('rep', 'ctx', 'tp'), parts along dimension 0, may hold values from -6 to 6
- rotated_new_keys: bfloat16 [8, 512, 1024], P('rep', 'ctx', 'tp'), parts along dimension 0, may hold values from -6 to 6
- incoming_values: bfloat16 [8, 512, 1024], P('rep', 'ctx', 'tp'), parts along dimension 0, may hold values from -6 to 6
- lengths: int32 [8], P('rep'), parts along dimension 0, may hold values from 8192 to 16384, as said below
- positions: int32 [8, 512], P('rep', 'ctx'), parts along dimension 0, may hold values from 8192 to 16895, as said below
Outputs:
- attended: bfloat16 [8, 512, 8192], P('rep', 'ctx', 'tp'), parts along dimension 0
The draws below stay inside these ranges and needn't reach their ends.
There are 4 independent parts, one for each index of `rep`. The reference program is written for one: setup_inputs(seed, part) draws one part's arguments, and reference() takes and returns one part's arrays. A program takes and returns all parts, laid end to end along the dimension named above; each array names one. Nothing has to cross between parts.
Inputs may be any that keep to these rules, and one draw needn't show every extreme that they name: `lengths`: one session of each part has all 16384 slots used. `positions`: along each session nondecreasing, the first equal to that session's entry of lengths, each next one equal or one more; a session with all 16384 slots used rises by one at every token.
All inputs are finite; a program needn't handle non-finite values.
Results may differ from the reference program's by a relative error of at most 0.0075.
Values may be sent and summed in bfloat16 or wider, within the bound.
No kernel may reach another device: no remote copies, remote signals or barrier semaphores. Data moves between devices by JAX's collectives and lax.ppermute only.
A program may use at most 64 MiB of HBM per device.

```python
import jax
import jax.numpy as jnp
from jax import lax

QUERY_HEADS = 64
KEY_VALUE_HEADS = 8
HEAD_SIZE = 128
SESSION_COUNT = 2
NEW_TOKEN_COUNT = 512
CACHE_SLOTS = 16384


def base_keys(key):
    unscaled_scores = jax.random.normal(jax.random.fold_in(key, 7), (SESSION_COUNT, CACHE_SLOTS, KEY_VALUE_HEADS, HEAD_SIZE), jnp.float32)
    return jnp.clip(unscaled_scores, -4.0, 4.0)


def session_lengths(key):
    base = jax.random.randint(jax.random.fold_in(key, 11), (SESSION_COUNT,), CACHE_SLOTS // 2, CACHE_SLOTS + 1)
    full = jax.random.randint(jax.random.fold_in(key, 12), (), 0, SESSION_COUNT)
    return jnp.where(jnp.arange(SESSION_COUNT) == full, CACHE_SLOTS, base).astype(jnp.int32)


def draw_cache_keys(key, part):
    joined_keys = base_keys(key)
    return joined_keys.reshape(SESSION_COUNT, CACHE_SLOTS, KEY_VALUE_HEADS * HEAD_SIZE).astype(jnp.bfloat16)


def draw_queries(key, part):
    own = jax.random.fold_in(key, 4)
    values = jnp.clip(2.5 * jax.random.normal(own, (SESSION_COUNT, NEW_TOKEN_COUNT, QUERY_HEADS, HEAD_SIZE), jnp.float32), -12.0, 12.0)
    return values.reshape(SESSION_COUNT, NEW_TOKEN_COUNT, QUERY_HEADS * HEAD_SIZE).astype(jnp.bfloat16)


def draw_lengths(key, part):
    return session_lengths(key)


def draw_positions(key, part):
    used = session_lengths(key)
    own = jax.random.fold_in(key, 5)
    steps = jax.random.randint(own, (SESSION_COUNT, NEW_TOKEN_COUNT), 0, 2)
    steps = jnp.where((used == CACHE_SLOTS)[:, None], 1, steps)
    steps = steps.at[:, 0].set(0)
    return (used[:, None] + jnp.cumsum(steps, axis=1)).astype(jnp.int32)


def level_of(stream_key, extent, split, low, high):
    level, own = 1.0, jax.random.fold_in(stream_key, 6)
    for position, shards_of in split:
        heights = jnp.exp(jax.random.uniform(jax.random.fold_in(own, position), (shards_of,), jnp.float32, low / len(split), high / len(split)))
        level = level * jnp.repeat(heights, extent[position] // shards_of).reshape([-1 if axis == position else 1 for axis in range(len(extent))])
    return level


def normal_values(rng, extent, deviation, reach, split=(), kind=jnp.bfloat16):
    array = deviation * jax.random.normal(rng, extent, jnp.float32)
    if split:
        array = array * level_of(rng, extent, split, -0.22, 0.18)
    return jnp.clip(array, -reach, reach).astype(kind)


def setup_inputs(seed: int = 0, part: int = 0) -> dict:
    key_list = jax.random.split(jax.random.key(seed), 8)
    own_keys = jax.random.split(jax.random.fold_in(key_list[7], part), 8)
    return {
        "queries": draw_queries(jax.random.fold_in(jax.random.fold_in(key_list[7], part), 71), part),
        "cache_keys": draw_cache_keys(jax.random.fold_in(jax.random.fold_in(key_list[7], part), 71), part),
        "stored_values": normal_values(own_keys[2], (SESSION_COUNT, CACHE_SLOTS, KEY_VALUE_HEADS * HEAD_SIZE), 1.0, 6.0, ((1, 16), (2, 8))),
        "rotated_new_keys": normal_values(own_keys[3], (SESSION_COUNT, NEW_TOKEN_COUNT, KEY_VALUE_HEADS * HEAD_SIZE), 1.0, 6.0, ((1, 16), (2, 8))),
        "incoming_values": normal_values(own_keys[4], (SESSION_COUNT, NEW_TOKEN_COUNT, KEY_VALUE_HEADS * HEAD_SIZE), 1.0, 6.0, ((1, 16), (2, 8))),
        "lengths": draw_lengths(jax.random.fold_in(jax.random.fold_in(key_list[7], part), 71), part),
        "positions": draw_positions(jax.random.fold_in(jax.random.fold_in(key_list[7], part), 71), part),
    }


NEG = -1e30


def reference(queries, cache_keys, stored_values, rotated_new_keys, incoming_values, lengths, positions):
    query_group = QUERY_HEADS // KEY_VALUE_HEADS
    scale = 1.0 / (HEAD_SIZE ** 0.5)
    results = []
    for session_index in range(SESSION_COUNT):
        query_rows = queries[session_index].astype(jnp.float32).reshape(NEW_TOKEN_COUNT, KEY_VALUE_HEADS, query_group, HEAD_SIZE).transpose(1, 0, 2, 3)
        joined_keys = jnp.concatenate([cache_keys[session_index], rotated_new_keys[session_index]], axis=0).astype(jnp.float32)
        joined_keys = joined_keys.reshape(CACHE_SLOTS + NEW_TOKEN_COUNT, KEY_VALUE_HEADS, HEAD_SIZE).transpose(1, 0, 2)
        joined_values = jnp.concatenate([stored_values[session_index], incoming_values[session_index]], axis=0).astype(jnp.float32)
        joined_values = joined_values.reshape(CACHE_SLOTS + NEW_TOKEN_COUNT, KEY_VALUE_HEADS, HEAD_SIZE).transpose(1, 0, 2)
        cache_ok = jnp.arange(CACHE_SLOTS, dtype=jnp.int32) < lengths[session_index]
        cache_ok = jnp.broadcast_to(cache_ok[None, :], (NEW_TOKEN_COUNT, CACHE_SLOTS))
        new_ok = positions[session_index][None, :] <= positions[session_index][:, None]
        mask = jnp.concatenate([cache_ok, new_ok], axis=1)[:, None, :]

        def head(args):
            qh, kh, vh = args
            scores = jnp.einsum('qgd,kd->qgk', qh, kh) * scale
            top = jnp.max(jnp.where(mask, scores, NEG), axis=-1)
            weights = jnp.where(mask, jnp.exp(scores - top[..., None]), 0.0)
            total = jnp.sum(weights, axis=-1)
            rounded = lax.optimization_barrier(weights.astype(jnp.bfloat16)).astype(jnp.float32)
            summed = jnp.einsum('qgk,kd->qgd', rounded, vh)
            return summed / total[..., None]

        out = lax.map(head, (query_rows, joined_keys, joined_values))
        results.append(out.transpose(1, 0, 2, 3).reshape(NEW_TOKEN_COUNT, QUERY_HEADS * HEAD_SIZE).astype(jnp.bfloat16))
    return jnp.stack(results)
```

```python
import functools

import jax
import jax.numpy as jnp
from jax import lax
from jax.experimental import pallas as pl
from jax.experimental.pallas import tpu as pltpu
from jax.sharding import PartitionSpec as P

HEAD = 128
NEG = -1e30
VMEM = pl.BlockSpec(memory_space=pltpu.VMEM)
SMEM = pl.BlockSpec(memory_space=pltpu.SMEM)
LIMIT = 48 * 1024 * 1024
PACK = 48 * 1024 * 1024
SCALE = 1.0 / HEAD**0.5


def swap(block, mask):
    count = lax.axis_size("ctx")
    return lax.ppermute(block, "ctx", [(i, i ^ mask) for i in range(count)])


def column(row, rows, period):
    r = lax.broadcasted_iota(jnp.int32, (rows, 128), 0) % period
    c = lax.broadcasted_iota(jnp.int32, (rows, 128), 1)
    spread = jnp.broadcast_to(row, (rows, 128))
    return jnp.sum(jnp.where(r == c, spread, 0.0), axis=1, keepdims=True)


def lane_row(spread):
    r = lax.broadcasted_iota(jnp.int32, (128, 128), 0)
    c = lax.broadcasted_iota(jnp.int32, (128, 128), 1)
    return jnp.sum(jnp.where(r == c, jnp.broadcast_to(spread, (128, 128)), 0.0), axis=0, keepdims=True)


def stat_block(lse):
    halves = jnp.concatenate([lane_row(lse[:128]), lane_row(lse[128:])], axis=0)
    hi = halves.astype(jnp.bfloat16).astype(jnp.float32)
    rest = halves - hi
    mid = rest.astype(jnp.bfloat16).astype(jnp.float32)
    low = rest - mid
    blank = jnp.zeros((10, 128), jnp.float32)
    return jnp.concatenate([hi, mid, low, blank], axis=0).astype(jnp.bfloat16)


def read_stats(block):
    block = block.astype(jnp.float32)
    halves = block[0:2] + block[2:4] + block[4:6]
    return jnp.concatenate([column(halves[0:1], 128, 128), column(halves[1:2], 128, 128)], axis=0)


def place_block(row):
    line = lax.broadcasted_iota(jnp.int32, (16, 128), 0)
    spread = jnp.broadcast_to(row, (16, 128))
    pieces = jnp.where(line == 0, spread >> 7, jnp.where(line == 1, spread & 127, 0))
    return pieces.astype(jnp.float32).astype(jnp.bfloat16)


def read_places(block):
    block = block.astype(jnp.float32)
    return block[0:1] * 128.0 + block[1:2]


def pack_queries_kernel(tokens, queries, places, out):
    sessions, size, _ = out.shape
    for s in range(sessions):
        for h in range((size - 16) // tokens):
            out[s, h * tokens : (h + 1) * tokens, :] = queries[s, :, h * HEAD : (h + 1) * HEAD]
        out[s, size - 16 : size, :] = place_block(places[s : s + 1, :])


def pack_queries(queries, places):
    sessions, tokens, width = queries.shape
    return pl.pallas_call(
        functools.partial(pack_queries_kernel, tokens),
        out_shape=jax.ShapeDtypeStruct((sessions, width // HEAD * tokens + 16, HEAD), jnp.bfloat16),
        in_specs=[VMEM] * 2,
        out_specs=VMEM,
        compiler_params=pltpu.CompilerParams(vmem_limit_bytes=LIMIT),
    )(queries, places)


def pack_keys_kernel(slots, fresh, places, k, v, nk, nv, out, keys, sems):
    nk_at = 2 * slots
    copies = [pltpu.make_async_copy(k, keys, sems.at[0])]
    for i, (ref, at, size) in enumerate(((v, slots, slots), (nk, nk_at, fresh), (nv, nk_at + fresh, fresh))):
        copies.append(pltpu.make_async_copy(ref, out.at[:, pl.ds(at, size)], sems.at[i + 1]))
    for copy in copies:
        copy.start()
    for s in range(out.shape[0]):
        out[s, nk_at + 2 * fresh : nk_at + 2 * fresh + 16, :] = place_block(places[s : s + 1, :])
    copies[0].wait()
    for s in range(out.shape[0]):
        for at in range(0, slots, HEAD):
            tile = keys[s, at : at + HEAD, :].astype(jnp.float32)
            out[s, at : at + HEAD, :] = tile.T.astype(jnp.bfloat16)
    for copy in copies[1:]:
        copy.wait()


def pack_keys(places, k, v, nk, nv):
    sessions, slots, _ = k.shape
    fresh = nk.shape[1]
    return pl.pallas_call(
        functools.partial(pack_keys_kernel, slots, fresh),
        out_shape=jax.ShapeDtypeStruct((sessions, 2 * (slots + fresh) + 16, HEAD), jnp.bfloat16),
        in_specs=[VMEM] + [pl.BlockSpec(memory_space=pltpu.HBM)] * 4,
        out_specs=VMEM,
        scratch_shapes=[pltpu.VMEM(k.shape, k.dtype), pltpu.SemaphoreType.DMA((4,))],
        compiler_params=pltpu.CompilerParams(vmem_limit_bytes=PACK),
    )(places, k, v, nk, nv)


def attend_kernel(scal, q, s0, s1, s2, s3, out, points, weights):
    blocks = (s0, s1, s2, s3)
    sessions, size, _ = q.shape
    rows = size - 16
    fresh = 128 // len(blocks)
    slots = (s0.shape[1] - 16) // 2 - fresh
    nk = 2 * slots
    keys = len(blocks) * slots + 128
    wide, tall = 256, 32
    lane = lax.broadcasted_iota(jnp.int32, (1, 128), 1)
    cells = lax.broadcasted_iota(jnp.int32, (1, wide), 1)
    nt = (((1,), (1,)), ((), ()))

    def score(s):
        mine = q[s, 0:rows, :]
        top = jnp.full((rows, 128), NEG, jnp.float32)
        for b, blk in enumerate(blocks):
            left = scal[s] - scal[sessions + b]
            for at in range(0, slots, wide):
                tiles = [blk[s, j : j + HEAD, :] for j in range(at, at + wide, HEAD)]
                got = jnp.dot(mine, jnp.concatenate(tiles, axis=1), preferred_element_type=jnp.float32)
                got = jnp.where(cells < left - at, got, NEG)
                points[s, :, b * slots + at : b * slots + at + wide] = got
                for j in range(0, wide, 128):
                    top = jnp.maximum(top, got[:, j : j + 128])
        qpos = column(read_places(q[s, rows:size, :]), rows, fresh)
        kpos = jnp.zeros((1, 128), jnp.float32)
        for b, blk in enumerate(blocks):
            places = read_places(blk[s, nk + 2 * fresh : nk + 2 * fresh + 16, :])
            kpos = jnp.where(lane // fresh == b, places, kpos)
        new_keys = jnp.concatenate([blk[s, nk : nk + fresh, :] for blk in blocks], axis=0)
        got = lax.dot_general(mine, new_keys, nt, preferred_element_type=jnp.float32)
        got = jnp.where(kpos <= qpos, got, NEG)
        points[s, :, keys - 128 : keys] = got
        return jnp.maximum(top, got)

    def weigh(s, top):
        shifts, totals = [], []
        for r in range(0, rows, tall):
            shift = jnp.max(top[r : r + tall, :], axis=1, keepdims=True) * SCALE
            total = jnp.zeros((tall, 128), jnp.float32)
            for at in range(0, keys, 512):
                end = min(at + 512, keys)
                w = jnp.exp(points[s, r : r + tall, at:end] * SCALE - shift)
                for j in range(0, end - at, 128):
                    total += w[:, j : j + 128]
                weights[s, r : r + tall, at:end] = w.astype(jnp.bfloat16)
            shifts.append(shift)
            totals.append(jnp.sum(total, axis=1, keepdims=True))
        return jnp.concatenate(shifts, axis=0), jnp.concatenate(totals, axis=0)

    def gather(s, shift, total):
        summed = jnp.zeros((rows, HEAD), jnp.float32)
        for b, blk in enumerate(blocks):
            w = weights[s, :, b * slots : (b + 1) * slots]
            summed += jnp.dot(w, blk[s, slots:nk, :], preferred_element_type=jnp.float32)
        new_values = jnp.concatenate([blk[s, nk + fresh : nk + 2 * fresh, :] for blk in blocks], axis=0)
        summed += jnp.dot(weights[s, :, keys - 128 : keys], new_values, preferred_element_type=jnp.float32)
        out[s, 0:rows, :] = (summed / total).astype(jnp.bfloat16)
        out[s, rows:size, :] = stat_block(shift + jnp.log(total))

    tops = [score(s) for s in range(sessions)]
    for s in range(sessions):
        gather(s, *weigh(s, tops[s]))


def attend(scal, q, blocks):
    sessions, size, _ = q.shape
    keys = len(blocks) * ((blocks[0].shape[1] - 16) // 2)
    return pl.pallas_call(
        attend_kernel,
        out_shape=jax.ShapeDtypeStruct(q.shape, jnp.bfloat16),
        in_specs=[SMEM] + [VMEM] * (1 + len(blocks)),
        out_specs=VMEM,
        scratch_shapes=[
            pltpu.VMEM((sessions, size - 16, keys), jnp.float32),
            pltpu.VMEM((sessions, size - 16, keys), jnp.bfloat16),
        ],
        compiler_params=pltpu.CompilerParams(vmem_limit_bytes=LIMIT),
        cost_estimate=pl.CostEstimate(flops=q.size, bytes_accessed=0, transcendentals=0),
    )(scal, q, *blocks)


def merged(rows, messages):
    logs = [read_stats(m[rows : rows + 16, :]) for m in messages]
    top = functools.reduce(jnp.maximum, logs)
    shares = [jnp.exp(x - top) for x in logs]
    total = sum(shares)
    value = sum(m[:rows, :].astype(jnp.float32) * (x / total) for m, x in zip(messages, shares))
    return value, top + jnp.log(total)


def merge_kernel(own, came, out):
    sessions, size, _ = own.shape
    rows = size - 16
    for s in range(sessions):
        value, lse = merged(rows, [own[s], came[s]])
        out[s, 0:rows, :] = value.astype(jnp.bfloat16)
        out[s, rows:size, :] = stat_block(lse)


def merge(own, came):
    return pl.pallas_call(
        merge_kernel,
        out_shape=jax.ShapeDtypeStruct(own.shape, jnp.bfloat16),
        in_specs=[VMEM, VMEM],
        out_specs=VMEM,
        compiler_params=pltpu.CompilerParams(vmem_limit_bytes=LIMIT),
    )(own, came)


def finish_kernel(one, two, three, out):
    sessions, tokens, width = out.shape
    rows = one.shape[1] - 16
    for s in range(sessions):
        value, _ = merged(rows, [one[s], two[s], three[s]])
        value = value.astype(jnp.bfloat16)
        for h in range(width // HEAD):
            out[s, :, h * HEAD : (h + 1) * HEAD] = value[h * tokens : (h + 1) * tokens, :]


def finish(one, two, three, tokens):
    sessions, size, _ = one.shape
    return pl.pallas_call(
        finish_kernel,
        out_shape=jax.ShapeDtypeStruct((sessions, tokens, (size - 16) // tokens * HEAD), jnp.bfloat16),
        in_specs=[VMEM] * 3,
        out_specs=VMEM,
        compiler_params=pltpu.CompilerParams(vmem_limit_bytes=LIMIT),
    )(one, two, three)


def per_device(queries, cache_keys, stored_values, new_keys, new_values, lengths, positions):
    member = lax.axis_index("ctx")
    tokens = queries.shape[1]
    slots = cache_keys.shape[1]
    places = jnp.tile(positions, (1, 128 // tokens))
    bases = jnp.stack([member, member ^ 1, member ^ 4, member ^ 5]) * slots
    scal = jnp.concatenate([lengths, bases]).astype(jnp.int32)

    near_q = pack_queries(queries, places)
    near_x = swap(near_q, 12)
    far_q = swap(near_q, 2)
    own = pack_keys(places, cache_keys, stored_values, new_keys, new_values)
    x_own = swap(own, 4)

    far_x = swap(far_q, 12)
    x_own, far_q, near_x = lax.optimization_barrier((x_own, far_q, near_x))
    blocks = (own, swap(own, 1), x_own, swap(x_own, 1))
    far_a = attend(scal, far_q, blocks)
    far_x, far_a = lax.optimization_barrier((far_x, far_a))
    far_b = attend(scal, far_x, blocks)
    far_came = swap(far_b, 12)
    far_b, near_x = lax.optimization_barrier((far_b, near_x))
    near_b = attend(scal, near_x, blocks)
    near_came = swap(near_b, 12)
    far_came, near_b, near_q = lax.optimization_barrier((far_came, near_b, near_q))
    far = merge(far_a, far_came)
    back = swap(far, 2)
    far, near_q = lax.optimization_barrier((far, near_q))
    near_a = attend(scal, near_q, blocks)
    return finish(near_a, near_came, back, tokens)


def solution(mesh):
    spec = P("rep", "ctx", "tp")
    return jax.shard_map(
        per_device,
        mesh=mesh,
        in_specs=(spec, spec, spec, spec, spec, P("rep"), P("rep", "ctx")),
        out_specs=spec,
        check_vma=False,
    )
```

```python
import functools

import jax
import jax.numpy as jnp
from jax import lax
from jax.experimental import pallas as pl
from jax.experimental.pallas import tpu as pltpu
from jax.sharding import PartitionSpec as P

HEAD = 128
NEG = -1e30
VMEM = pl.BlockSpec(memory_space=pltpu.VMEM)
SMEM = pl.BlockSpec(memory_space=pltpu.SMEM)
LIMIT = 48 * 1024 * 1024
PACK = 48 * 1024 * 1024
SCALE = 1.0 / HEAD**0.5


def swap(block, mask):
    count = lax.axis_size("ctx")
    return lax.ppermute(block, "ctx", [(i, i ^ mask) for i in range(count)])


def column(row, rows, period):
    r = lax.broadcasted_iota(jnp.int32, (rows, 128), 0) % period
    c = lax.broadcasted_iota(jnp.int32, (rows, 128), 1)
    spread = jnp.broadcast_to(row, (rows, 128))
    return jnp.sum(jnp.where(r == c, spread, 0.0), axis=1, keepdims=True)


def lane_row(spread):
    r = lax.broadcasted_iota(jnp.int32, (128, 128), 0)
    c = lax.broadcasted_iota(jnp.int32, (128, 128), 1)
    return jnp.sum(jnp.where(r == c, jnp.broadcast_to(spread, (128, 128)), 0.0), axis=0, keepdims=True)


def stat_block(lse):
    halves = jnp.concatenate([lane_row(lse[:128]), lane_row(lse[128:])], axis=0)
    hi = halves.astype(jnp.bfloat16).astype(jnp.float32)
    rest = halves - hi
    mid = rest.astype(jnp.bfloat16).astype(jnp.float32)
    low = rest - mid
    blank = jnp.zeros((10, 128), jnp.float32)
    return jnp.concatenate([hi, mid, low, blank], axis=0).astype(jnp.bfloat16)


def read_stats(block):
    block = block.astype(jnp.float32)
    halves = block[0:2] + block[2:4] + block[4:6]
    return jnp.concatenate([column(halves[0:1], 128, 128), column(halves[1:2], 128, 128)], axis=0)


def place_block(row):
    shape = (16, row.shape[1])
    line = lax.broadcasted_iota(jnp.int32, shape, 0)
    spread = jnp.broadcast_to(row, shape)
    pieces = jnp.where(line == 0, spread >> 7, jnp.where(line == 1, spread & 127, 0))
    return pieces.astype(jnp.float32).astype(jnp.bfloat16)


def put_places(out, s, at, places):
    out[s, at : at + 16, :] = jnp.zeros((16, HEAD), jnp.bfloat16)
    out[s, at : at + 16, 0 : places.shape[1]] = place_block(places[s : s + 1, :])


def read_places(block):
    block = block.astype(jnp.float32)
    return block[0:1] * 128.0 + block[1:2]


def pack_queries_kernel(tokens, queries, places, out):
    sessions, size, _ = out.shape
    for s in range(sessions):
        for h in range((size - 16) // tokens):
            out[s, h * tokens : (h + 1) * tokens, :] = queries[s, :, h * HEAD : (h + 1) * HEAD]
        put_places(out, s, size - 16, places)


def pack_queries(queries, places):
    sessions, tokens, width = queries.shape
    return pl.pallas_call(
        functools.partial(pack_queries_kernel, tokens),
        out_shape=jax.ShapeDtypeStruct((sessions, width // HEAD * tokens + 16, HEAD), jnp.bfloat16),
        in_specs=[VMEM] * 2,
        out_specs=VMEM,
        compiler_params=pltpu.CompilerParams(vmem_limit_bytes=LIMIT),
    )(queries, places)


def pack_keys_kernel(slots, fresh, places, k, v, nk, nv, out, spots, sems):
    copies = [pltpu.make_async_copy(places, spots, sems.at[4])]
    at = 0
    for i, (ref, size) in enumerate(((k, slots), (v, slots), (nk, fresh), (nv, fresh))):
        copies.append(pltpu.make_async_copy(ref, out.at[:, pl.ds(at, size)], sems.at[i]))
        at += size
    for copy in copies:
        copy.start()
    copies[0].wait()
    for s in range(out.shape[0]):
        put_places(out, s, at, spots)
    for copy in copies[1:]:
        copy.wait()


def pack_keys(places, k, v, nk, nv):
    sessions, slots, _ = k.shape
    fresh = nk.shape[1]
    shape = (sessions, 2 * (slots + fresh) + 16, HEAD)
    return pl.pallas_call(
        functools.partial(pack_keys_kernel, slots, fresh),
        out_shape=pltpu.VMEM(shape, jnp.bfloat16),
        in_specs=[pl.BlockSpec(memory_space=pltpu.HBM)] * 5,
        out_specs=VMEM,
        scratch_shapes=[pltpu.VMEM(places.shape, places.dtype), pltpu.SemaphoreType.DMA((5,))],
        compiler_params=pltpu.CompilerParams(vmem_limit_bytes=PACK),
    )(*(pltpu.with_memory_space_constraint(x, pltpu.HBM) for x in (places, k, v, nk, nv)))


def attend_kernel(scal, q, s0, s1, s2, s3, out):
    blocks = (s0, s1, s2, s3)
    sessions, size, _ = q.shape
    rows = size - 16
    fresh = 128 // len(blocks)
    slots = (s0.shape[1] - 16) // 2 - fresh
    nk = 2 * slots
    cells = lax.broadcasted_iota(jnp.int32, (1, slots), 1)
    nt = (((1,), (1,)), ((), ()))
    for s in range(sessions):
        mine = q[s, 0:rows, :]
        qpos = column(read_places(q[s, rows:size, :]), rows, fresh)
        kpos = [read_places(blk[s, nk + 2 * fresh : nk + 2 * fresh + 16, :])[:, 0:fresh] for blk in blocks]
        scores = []
        for b, blk in enumerate(blocks):
            got = lax.dot_general(mine, blk[s, 0:slots, :], nt, preferred_element_type=jnp.float32)
            scores.append(jnp.where(cells < scal[s] - scal[sessions + b], got, NEG))
        new_keys = jnp.concatenate([blk[s, nk : nk + fresh, :] for blk in blocks], axis=0)
        got = lax.dot_general(mine, new_keys, nt, preferred_element_type=jnp.float32)
        scores.append(jnp.where(jnp.concatenate(kpos, axis=1) <= qpos, got, NEG))
        values = [blk[s, slots:nk, :] for blk in blocks]
        values.append(jnp.concatenate([blk[s, nk + fresh : nk + 2 * fresh, :] for blk in blocks], axis=0))
        shift = SCALE * functools.reduce(jnp.maximum, [jnp.max(x, axis=1, keepdims=True) for x in scores])
        total = jnp.zeros((rows, 1), jnp.float32)
        summed = jnp.zeros((rows, HEAD), jnp.float32)
        for x, v in zip(scores, values):
            w = jnp.exp(x * SCALE - shift)
            total += jnp.sum(w, axis=1, keepdims=True)
            summed += jnp.dot(w.astype(jnp.bfloat16), v, preferred_element_type=jnp.float32)
        out[s, 0:rows, :] = (summed / total).astype(jnp.bfloat16)
        out[s, rows:size, :] = stat_block(shift + jnp.log(total))


def attend(scal, q, blocks):
    return pl.pallas_call(
        attend_kernel,
        out_shape=jax.ShapeDtypeStruct(q.shape, jnp.bfloat16),
        in_specs=[SMEM] + [VMEM] * (1 + len(blocks)),
        out_specs=VMEM,
        compiler_params=pltpu.CompilerParams(vmem_limit_bytes=LIMIT),
        cost_estimate=pl.CostEstimate(flops=q.size, bytes_accessed=0, transcendentals=0),
    )(scal, q, *blocks)


def merged(rows, messages):
    logs = [read_stats(m[rows : rows + 16, :]) for m in messages]
    top = functools.reduce(jnp.maximum, logs)
    shares = [jnp.exp(x - top) for x in logs]
    total = sum(shares)
    value = sum(m[:rows, :].astype(jnp.float32) * (x / total) for m, x in zip(messages, shares))
    return value, top + jnp.log(total)


def merge_kernel(own, came, out):
    sessions, size, _ = own.shape
    rows = size - 16
    for s in range(sessions):
        value, lse = merged(rows, [own[s], came[s]])
        out[s, 0:rows, :] = value.astype(jnp.bfloat16)
        out[s, rows:size, :] = stat_block(lse)
        out[s, size:, :] = jnp.zeros((out.shape[1] - size, HEAD), jnp.bfloat16)


def merge(own, came):
    sessions, size, _ = own.shape
    return pl.pallas_call(
        merge_kernel,
        out_shape=jax.ShapeDtypeStruct((sessions, size + 16, HEAD), jnp.bfloat16),
        in_specs=[VMEM, VMEM],
        out_specs=VMEM,
        compiler_params=pltpu.CompilerParams(vmem_limit_bytes=LIMIT),
    )(own, came)


def finish_kernel(one, two, three, out):
    sessions, tokens, width = out.shape
    rows = one.shape[1] - 16
    for s in range(sessions):
        value, _ = merged(rows, [one[s], two[s], three[s]])
        value = value.astype(jnp.bfloat16)
        for h in range(width // HEAD):
            out[s, :, h * HEAD : (h + 1) * HEAD] = value[h * tokens : (h + 1) * tokens, :]


def finish(one, two, three, tokens):
    sessions, size, _ = one.shape
    return pl.pallas_call(
        finish_kernel,
        out_shape=jax.ShapeDtypeStruct((sessions, tokens, (size - 16) // tokens * HEAD), jnp.bfloat16),
        in_specs=[VMEM] * 3,
        out_specs=VMEM,
        compiler_params=pltpu.CompilerParams(vmem_limit_bytes=LIMIT),
    )(one, two, three)


def per_device(queries, cache_keys, stored_values, new_keys, new_values, lengths, positions):
    member = lax.axis_index("ctx")
    tokens = queries.shape[1]
    slots = cache_keys.shape[1]
    bases = jnp.stack([member, member ^ 1, member ^ 4, member ^ 5]) * slots
    scal = jnp.concatenate([lengths, bases]).astype(jnp.int32)

    near_q = pack_queries(queries, positions)
    near_x = [swap(near_q[s], 12) for s in range(near_q.shape[0])]
    far_q = swap(near_q, 2)
    own = pack_keys(positions, cache_keys, stored_values, new_keys, new_values)
    x_own = swap(own, 4)
    pair = swap(own, 1)
    far_q, scal, *near_x = lax.optimization_barrier((far_q, scal, *near_x))
    far_x = swap(far_q, 12)
    x_own, far_x = lax.optimization_barrier((x_own, far_x))
    blocks = (own, pair, x_own, swap(x_own, 1))

    far_b = attend(scal, far_x, blocks)
    far_came = swap(far_b, 12)
    far_b, far_q = lax.optimization_barrier((far_b, far_q))
    far_a = attend(scal, far_q, blocks)
    far_came, far_a = lax.optimization_barrier((far_came, far_a))
    far = merge(far_a, far_came)
    back = swap(far, 2)

    far, near_q, *near_x = lax.optimization_barrier((far, near_q, *near_x))
    near_b = attend(scal, jnp.stack(near_x), blocks)
    near_came = swap(near_b, 12)
    near_b, near_q = lax.optimization_barrier((near_b, near_q))
    near_a = attend(scal, near_q, blocks)
    return finish(near_a, near_came, back, tokens)


def solution(mesh):
    spec = P("rep", "ctx", "tp")
    return jax.shard_map(
        per_device,
        mesh=mesh,
        in_specs=(spec, spec, spec, spec, spec, P("rep"), P("rep", "ctx")),
        out_specs=spec,
        check_vma=False,
    )
```

```python
import functools

import jax
import jax.numpy as jnp
from jax import lax
from jax.experimental import pallas as pl
from jax.experimental.pallas import tpu as pltpu
from jax.sharding import PartitionSpec as P

HEAD = 128
NEG = -1e30
VMEM = pl.BlockSpec(memory_space=pltpu.VMEM)
SMEM = pl.BlockSpec(memory_space=pltpu.SMEM)
LIMIT = 48 * 1024 * 1024
PACK = 48 * 1024 * 1024
SCALE = 1.0 / HEAD**0.5


def swap(block, mask):
    count = lax.axis_size("ctx")
    return lax.ppermute(block, "ctx", [(i, i ^ mask) for i in range(count)])


def column(row, rows, period):
    r = lax.broadcasted_iota(jnp.int32, (rows, 128), 0) % period
    c = lax.broadcasted_iota(jnp.int32, (rows, 128), 1)
    spread = jnp.broadcast_to(row, (rows, 128))
    return jnp.sum(jnp.where(r == c, spread, 0.0), axis=1, keepdims=True)


def lane_row(spread):
    r = lax.broadcasted_iota(jnp.int32, (128, 128), 0)
    c = lax.broadcasted_iota(jnp.int32, (128, 128), 1)
    return jnp.sum(jnp.where(r == c, jnp.broadcast_to(spread, (128, 128)), 0.0), axis=0, keepdims=True)


def stat_block(lse):
    halves = jnp.concatenate([lane_row(lse[:128]), lane_row(lse[128:])], axis=0)
    hi = halves.astype(jnp.bfloat16).astype(jnp.float32)
    rest = halves - hi
    mid = rest.astype(jnp.bfloat16).astype(jnp.float32)
    low = rest - mid
    blank = jnp.zeros((10, 128), jnp.float32)
    return jnp.concatenate([hi, mid, low, blank], axis=0).astype(jnp.bfloat16)


def read_stats(block):
    block = block.astype(jnp.float32)
    halves = block[0:2] + block[2:4] + block[4:6]
    return jnp.concatenate([column(halves[0:1], 128, 128), column(halves[1:2], 128, 128)], axis=0)


def place_block(row):
    shape = (16, row.shape[1])
    line = lax.broadcasted_iota(jnp.int32, shape, 0)
    spread = jnp.broadcast_to(row, shape)
    pieces = jnp.where(line == 0, spread >> 7, jnp.where(line == 1, spread & 127, 0))
    return pieces.astype(jnp.float32).astype(jnp.bfloat16)


def put_places(out, s, at, places):
    out[s, at : at + 16, :] = jnp.zeros((16, HEAD), jnp.bfloat16)
    out[s, at : at + 16, 0 : places.shape[1]] = place_block(places[s : s + 1, :])


def read_places(block):
    block = block.astype(jnp.float32)
    return block[0:1] * 128.0 + block[1:2]


def pack_queries_kernel(tokens, queries, places, out):
    sessions, size, _ = out.shape
    for s in range(sessions):
        for h in range((size - 16) // tokens):
            out[s, h * tokens : (h + 1) * tokens, :] = queries[s, :, h * HEAD : (h + 1) * HEAD]
        put_places(out, s, size - 16, places)


def pack_queries(queries, places):
    sessions, tokens, width = queries.shape
    return pl.pallas_call(
        functools.partial(pack_queries_kernel, tokens),
        out_shape=jax.ShapeDtypeStruct((sessions, width // HEAD * tokens + 16, HEAD), jnp.bfloat16),
        in_specs=[VMEM] * 2,
        out_specs=VMEM,
        compiler_params=pltpu.CompilerParams(vmem_limit_bytes=LIMIT),
    )(queries, places)


def pack_keys_kernel(slots, fresh, places, k, v, nk, nv, out, spots, sems):
    copies = [pltpu.make_async_copy(places, spots, sems.at[4])]
    at = 0
    for i, (ref, size) in enumerate(((k, slots), (v, slots), (nk, fresh), (nv, fresh))):
        copies.append(pltpu.make_async_copy(ref, out.at[:, pl.ds(at, size)], sems.at[i]))
        at += size
    for copy in copies:
        copy.start()
    copies[0].wait()
    for s in range(out.shape[0]):
        put_places(out, s, at, spots)
    for copy in copies[1:]:
        copy.wait()


def pack_keys(places, k, v, nk, nv):
    sessions, slots, _ = k.shape
    fresh = nk.shape[1]
    shape = (sessions, 2 * (slots + fresh) + 16, HEAD)
    return pl.pallas_call(
        functools.partial(pack_keys_kernel, slots, fresh),
        out_shape=pltpu.VMEM(shape, jnp.bfloat16),
        in_specs=[pl.BlockSpec(memory_space=pltpu.HBM)] * 5,
        out_specs=VMEM,
        scratch_shapes=[pltpu.VMEM(places.shape, places.dtype), pltpu.SemaphoreType.DMA((5,))],
        compiler_params=pltpu.CompilerParams(vmem_limit_bytes=PACK),
    )(*(pltpu.with_memory_space_constraint(x, pltpu.HBM) for x in (places, k, v, nk, nv)))


def attend_kernel(scal, q, s0, s1, s2, s3, out):
    blocks = (s0, s1, s2, s3)
    sessions, size, _ = q.shape
    rows = size - 16
    fresh = 128 // len(blocks)
    slots = (s0.shape[1] - 16) // 2 - fresh
    nk = 2 * slots
    cells = lax.broadcasted_iota(jnp.int32, (1, slots), 1)
    nt = (((1,), (1,)), ((), ()))
    left = [[scal[s] - scal[sessions + b] for b in range(len(blocks))] for s in range(sessions)]

    def score(s, b, masked):
        mine = q[s, 0:rows, :]
        if b < len(blocks):
            got = lax.dot_general(mine, blocks[b][s, 0:slots, :], nt, preferred_element_type=jnp.float32)
            return jnp.where(cells < left[s][b], got, NEG) if masked else got
        qpos = column(read_places(q[s, rows:size, :]), rows, fresh)
        kpos = [read_places(blk[s, nk + 2 * fresh : nk + 2 * fresh + 16, :])[:, 0:fresh] for blk in blocks]
        new_keys = jnp.concatenate([blk[s, nk : nk + fresh, :] for blk in blocks], axis=0)
        got = lax.dot_general(mine, new_keys, nt, preferred_element_type=jnp.float32)
        return jnp.where(jnp.concatenate(kpos, axis=1) <= qpos, got, NEG)

    def weigh(s, b, got, state):
        shift = jnp.max(got, axis=1, keepdims=True) * SCALE
        if state is not None:
            shift = jnp.maximum(shift, state[0])
        w = jnp.exp(got * SCALE - shift)
        total = jnp.sum(w, axis=1, keepdims=True)
        if b < len(blocks):
            v = blocks[b][s, slots:nk, :]
        else:
            v = jnp.concatenate([blk[s, nk + fresh : nk + 2 * fresh, :] for blk in blocks], axis=0)
        summed = jnp.dot(w.astype(jnp.bfloat16), v, preferred_element_type=jnp.float32)
        if state is not None:
            scale = jnp.exp(state[0] - shift)
            total += scale * state[1]
            summed += scale * state[2]
        return shift, total, summed

    def body(masked):
        units = [(s, b) for b in (len(blocks), *range(len(blocks))) for s in range(sessions)]
        states = [None] * sessions
        ahead = score(*units[0], masked)
        for n, (s, b) in enumerate(units):
            got = ahead
            if n + 1 < len(units):
                ahead = score(*units[n + 1], masked)
            states[s] = weigh(s, b, got, states[s])
        for s, (shift, total, summed) in enumerate(states):
            out[s, 0:rows, :] = (summed / total).astype(jnp.bfloat16)
            out[s, rows:size, :] = stat_block(shift + jnp.log(total))

    full = functools.reduce(jnp.logical_and, [x >= slots for row in left for x in row])
    pl.when(full)(lambda: body(False))
    pl.when(jnp.logical_not(full))(lambda: body(True))


def attend(scal, q, blocks):
    return pl.pallas_call(
        attend_kernel,
        out_shape=jax.ShapeDtypeStruct(q.shape, jnp.bfloat16),
        in_specs=[SMEM] + [VMEM] * (1 + len(blocks)),
        out_specs=VMEM,
        compiler_params=pltpu.CompilerParams(vmem_limit_bytes=LIMIT),
        cost_estimate=pl.CostEstimate(flops=q.size, bytes_accessed=0, transcendentals=0),
    )(scal, q, *blocks)


def merged(rows, messages):
    logs = [read_stats(m[rows : rows + 16, :]) for m in messages]
    top = functools.reduce(jnp.maximum, logs)
    shares = [jnp.exp(x - top) for x in logs]
    total = sum(shares)
    value = sum(m[:rows, :].astype(jnp.float32) * (x / total) for m, x in zip(messages, shares))
    return value, top + jnp.log(total)


def merge_kernel(own, came, out):
    sessions, size, _ = own.shape
    rows = size - 16
    for s in range(sessions):
        value, lse = merged(rows, [own[s], came[s]])
        out[s, 0:rows, :] = value.astype(jnp.bfloat16)
        out[s, rows:size, :] = stat_block(lse)
        out[s, size:, :] = jnp.zeros((out.shape[1] - size, HEAD), jnp.bfloat16)


def merge(own, came):
    sessions, size, _ = own.shape
    return pl.pallas_call(
        merge_kernel,
        out_shape=jax.ShapeDtypeStruct((sessions, size + 16, HEAD), jnp.bfloat16),
        in_specs=[VMEM, VMEM],
        out_specs=VMEM,
        compiler_params=pltpu.CompilerParams(vmem_limit_bytes=LIMIT),
    )(own, came)


def finish_kernel(one, two, three, out):
    sessions, tokens, width = out.shape
    rows = one.shape[1] - 16
    for s in range(sessions):
        value, _ = merged(rows, [one[s], two[s], three[s]])
        value = value.astype(jnp.bfloat16)
        for h in range(width // HEAD):
            out[s, :, h * HEAD : (h + 1) * HEAD] = value[h * tokens : (h + 1) * tokens, :]


def finish(one, two, three, tokens):
    sessions, size, _ = one.shape
    return pl.pallas_call(
        finish_kernel,
        out_shape=jax.ShapeDtypeStruct((sessions, tokens, (size - 16) // tokens * HEAD), jnp.bfloat16),
        in_specs=[VMEM] * 3,
        out_specs=VMEM,
        compiler_params=pltpu.CompilerParams(vmem_limit_bytes=LIMIT),
    )(one, two, three)


def per_device(queries, cache_keys, stored_values, new_keys, new_values, lengths, positions):
    member = lax.axis_index("ctx")
    tokens = queries.shape[1]
    slots = cache_keys.shape[1]
    bases = jnp.stack([member, member ^ 1, member ^ 4, member ^ 5]) * slots
    scal = jnp.concatenate([lengths, bases]).astype(jnp.int32)

    near_q = pack_queries(queries, positions)
    near_x = [swap(near_q[s], 12) for s in range(near_q.shape[0])]
    far_q = swap(near_q, 2)
    own = pack_keys(positions, cache_keys, stored_values, new_keys, new_values)
    x_own = swap(own, 4)
    pair = swap(own, 1)
    far_q, scal, *near_x = lax.optimization_barrier((far_q, scal, *near_x))
    far_x = swap(far_q, 12)
    x_own, far_x = lax.optimization_barrier((x_own, far_x))
    blocks = (own, pair, x_own, swap(x_own, 1))

    far_b = attend(scal, far_x, blocks)
    far_came = swap(far_b, 12)
    far_b, far_q = lax.optimization_barrier((far_b, far_q))
    far_a = attend(scal, far_q, blocks)
    far_came, far_a = lax.optimization_barrier((far_came, far_a))
    far = merge(far_a, far_came)
    back = swap(far, 2)

    far, near_q, *near_x = lax.optimization_barrier((far, near_q, *near_x))
    near_b = attend(scal, jnp.stack(near_x), blocks)
    near_came = swap(near_b, 12)
    near_b, near_q = lax.optimization_barrier((near_b, near_q))
    near_a = attend(scal, near_q, blocks)
    return finish(near_a, near_came, back, tokens)


def solution(mesh):
    spec = P("rep", "ctx", "tp")
    return jax.shard_map(
        per_device,
        mesh=mesh,
        in_specs=(spec, spec, spec, spec, spec, P("rep"), P("rep", "ctx")),
        out_specs=spec,
        check_vma=False,
    )
```

```python
import functools

import jax
import jax.numpy as jnp
from jax import lax
from jax.experimental import pallas as pl
from jax.experimental.pallas import tpu as pltpu
from jax.sharding import PartitionSpec as P

HEAD = 128
NEG = -1e30
VMEM = pl.BlockSpec(memory_space=pltpu.VMEM)
SMEM = pl.BlockSpec(memory_space=pltpu.SMEM)
LIMIT = 48 * 1024 * 1024
STEER = 16000000000
PACK = 48 * 1024 * 1024
SCALE = 1.0 / HEAD**0.5


def swap(block, mask):
    count = lax.axis_size("ctx")
    return lax.ppermute(block, "ctx", [(i, i ^ mask) for i in range(count)])


def column(row, rows, period):
    r = lax.broadcasted_iota(jnp.int32, (rows, 128), 0) % period
    c = lax.broadcasted_iota(jnp.int32, (rows, 128), 1)
    spread = jnp.broadcast_to(row, (rows, 128))
    return jnp.sum(jnp.where(r == c, spread, 0.0), axis=1, keepdims=True)


def lane_row(spread):
    r = lax.broadcasted_iota(jnp.int32, (128, 128), 0)
    c = lax.broadcasted_iota(jnp.int32, (128, 128), 1)
    return jnp.sum(jnp.where(r == c, jnp.broadcast_to(spread, (128, 128)), 0.0), axis=0, keepdims=True)


def stat_block(lse):
    halves = jnp.concatenate([lane_row(lse[:128]), lane_row(lse[128:])], axis=0)
    hi = halves.astype(jnp.bfloat16).astype(jnp.float32)
    rest = halves - hi
    mid = rest.astype(jnp.bfloat16).astype(jnp.float32)
    low = rest - mid
    blank = jnp.zeros((10, 128), jnp.float32)
    return jnp.concatenate([hi, mid, low, blank], axis=0).astype(jnp.bfloat16)


def read_stats(block):
    block = block.astype(jnp.float32)
    halves = block[0:2] + block[2:4] + block[4:6]
    return jnp.concatenate([column(halves[0:1], 128, 128), column(halves[1:2], 128, 128)], axis=0)


def place_block(row):
    shape = (16, row.shape[1])
    line = lax.broadcasted_iota(jnp.int32, shape, 0)
    spread = jnp.broadcast_to(row, shape)
    pieces = jnp.where(line == 0, spread >> 7, jnp.where(line == 1, spread & 127, 0))
    return pieces.astype(jnp.float32).astype(jnp.bfloat16)


def put_places(out, s, at, places):
    out[s, at : at + 16, :] = jnp.zeros((16, HEAD), jnp.bfloat16)
    out[s, at : at + 16, 0 : places.shape[1]] = place_block(places[s : s + 1, :])


def read_places(block):
    block = block.astype(jnp.float32)
    return block[0:1] * 128.0 + block[1:2]


def pack_queries_kernel(tokens, queries, places, out):
    sessions, size, _ = out.shape
    for s in range(sessions):
        for h in range((size - 16) // tokens):
            out[s, h * tokens : (h + 1) * tokens, :] = queries[s, :, h * HEAD : (h + 1) * HEAD]
        put_places(out, s, size - 16, places)


def pack_queries(queries, places):
    sessions, tokens, width = queries.shape
    return pl.pallas_call(
        functools.partial(pack_queries_kernel, tokens),
        out_shape=jax.ShapeDtypeStruct((sessions, width // HEAD * tokens + 16, HEAD), jnp.bfloat16),
        in_specs=[VMEM] * 2,
        out_specs=VMEM,
        compiler_params=pltpu.CompilerParams(vmem_limit_bytes=LIMIT),
    )(queries, places)


def pack_keys_kernel(slots, fresh, places, k, v, nk, nv, out, spots, sems):
    copies = [pltpu.make_async_copy(places, spots, sems.at[4])]
    at = 0
    for i, (ref, size) in enumerate(((k, slots), (v, slots), (nk, fresh), (nv, fresh))):
        copies.append(pltpu.make_async_copy(ref, out.at[:, pl.ds(at, size)], sems.at[i]))
        at += size
    for copy in copies:
        copy.start()
    copies[0].wait()
    for s in range(out.shape[0]):
        put_places(out, s, at, spots)
    for copy in copies[1:]:
        copy.wait()


def pack_keys(places, k, v, nk, nv):
    sessions, slots, _ = k.shape
    fresh = nk.shape[1]
    shape = (sessions, 2 * (slots + fresh) + 16, HEAD)
    return pl.pallas_call(
        functools.partial(pack_keys_kernel, slots, fresh),
        out_shape=pltpu.VMEM(shape, jnp.bfloat16),
        in_specs=[pl.BlockSpec(memory_space=pltpu.HBM)] * 5,
        out_specs=VMEM,
        scratch_shapes=[pltpu.VMEM(places.shape, places.dtype), pltpu.SemaphoreType.DMA((5,))],
        compiler_params=pltpu.CompilerParams(vmem_limit_bytes=PACK),
    )(*(pltpu.with_memory_space_constraint(x, pltpu.HBM) for x in (places, k, v, nk, nv)))


def attend_kernel(scal, q, s0, s1, s2, s3, out):
    blocks = (s0, s1, s2, s3)
    sessions, size, _ = q.shape
    rows = size - 16
    fresh = 128 // len(blocks)
    slots = (s0.shape[1] - 16) // 2 - fresh
    nk = 2 * slots
    cells = lax.broadcasted_iota(jnp.int32, (1, slots), 1)
    nt = (((1,), (1,)), ((), ()))
    left = [[scal[s] - scal[sessions + b] for b in range(len(blocks))] for s in range(sessions)]

    def score(s, b, masked):
        mine = q[s, 0:rows, :]
        if b < len(blocks):
            got = lax.dot_general(mine, blocks[b][s, 0:slots, :], nt, preferred_element_type=jnp.float32)
            return jnp.where(cells < left[s][b], got, NEG) if masked else got
        qpos = column(read_places(q[s, rows:size, :]), rows, fresh)
        kpos = [read_places(blk[s, nk + 2 * fresh : nk + 2 * fresh + 16, :])[:, 0:fresh] for blk in blocks]
        new_keys = jnp.concatenate([blk[s, nk : nk + fresh, :] for blk in blocks], axis=0)
        got = lax.dot_general(mine, new_keys, nt, preferred_element_type=jnp.float32)
        return jnp.where(jnp.concatenate(kpos, axis=1) <= qpos, got, NEG)

    def weigh(s, b, got, state):
        shift = jnp.max(got, axis=1, keepdims=True) * SCALE
        if state is not None:
            shift = jnp.maximum(shift, state[0])
        w = jnp.exp(got * SCALE - shift)
        total = jnp.sum(w, axis=1, keepdims=True)
        if b < len(blocks):
            v = blocks[b][s, slots:nk, :]
        else:
            v = jnp.concatenate([blk[s, nk + fresh : nk + 2 * fresh, :] for blk in blocks], axis=0)
        summed = jnp.dot(w.astype(jnp.bfloat16), v, preferred_element_type=jnp.float32)
        if state is not None:
            scale = jnp.exp(state[0] - shift)
            total += scale * state[1]
            summed += scale * state[2]
        return shift, total, summed

    def body(masked):
        units = [(s, b) for b in (len(blocks), *range(len(blocks))) for s in range(sessions)]
        states = [None] * sessions
        ahead = score(*units[0], masked)
        for n, (s, b) in enumerate(units):
            got = ahead
            if n + 1 < len(units):
                ahead = score(*units[n + 1], masked)
            states[s] = weigh(s, b, got, states[s])
        for s, (shift, total, summed) in enumerate(states):
            out[s, 0:rows, :] = (summed / total).astype(jnp.bfloat16)
            out[s, rows:size, :] = stat_block(shift + jnp.log(total))

    full = functools.reduce(jnp.logical_and, [x >= slots for row in left for x in row])
    pl.when(full)(lambda: body(False))
    pl.when(jnp.logical_not(full))(lambda: body(True))


def attend(scal, q, blocks):
    return pl.pallas_call(
        attend_kernel,
        out_shape=jax.ShapeDtypeStruct(q.shape, jnp.bfloat16),
        in_specs=[SMEM] + [VMEM] * (1 + len(blocks)),
        out_specs=VMEM,
        compiler_params=pltpu.CompilerParams(vmem_limit_bytes=LIMIT),
        cost_estimate=pl.CostEstimate(flops=q.size, bytes_accessed=0, transcendentals=0),
    )(scal, q, *blocks)


def pass_on_kernel(came, out):
    out[...] = came[...]


def pass_on(came):
    return pl.pallas_call(
        pass_on_kernel,
        out_shape=jax.ShapeDtypeStruct(came.shape, came.dtype),
        in_specs=[VMEM],
        out_specs=VMEM,
        compiler_params=pltpu.CompilerParams(vmem_limit_bytes=LIMIT),
        cost_estimate=pl.CostEstimate(flops=STEER, bytes_accessed=0, transcendentals=0),
    )(came)


def merged(rows, messages):
    logs = [read_stats(m[rows : rows + 16, :]) for m in messages]
    top = functools.reduce(jnp.maximum, logs)
    shares = [jnp.exp(x - top) for x in logs]
    total = sum(shares)
    value = sum(m[:rows, :].astype(jnp.float32) * (x / total) for m, x in zip(messages, shares))
    return value, top + jnp.log(total)


def merge_kernel(own, came, out):
    sessions, size, _ = own.shape
    rows = size - 16
    for s in range(sessions):
        value, lse = merged(rows, [own[s], came[s]])
        out[s, 0:rows, :] = value.astype(jnp.bfloat16)
        out[s, rows:size, :] = stat_block(lse)
        out[s, size:, :] = jnp.zeros((out.shape[1] - size, HEAD), jnp.bfloat16)


def merge(own, came):
    sessions, size, _ = own.shape
    return pl.pallas_call(
        merge_kernel,
        out_shape=jax.ShapeDtypeStruct((sessions, size + 16, HEAD), jnp.bfloat16),
        in_specs=[VMEM, VMEM],
        out_specs=VMEM,
        compiler_params=pltpu.CompilerParams(vmem_limit_bytes=LIMIT),
    )(own, came)


def finish_kernel(one, two, three, out):
    sessions, tokens, width = out.shape
    rows = one.shape[1] - 16
    for s in range(sessions):
        value, _ = merged(rows, [one[s], two[s], three[s]])
        value = value.astype(jnp.bfloat16)
        for h in range(width // HEAD):
            out[s, :, h * HEAD : (h + 1) * HEAD] = value[h * tokens : (h + 1) * tokens, :]


def finish(one, two, three, tokens):
    sessions, size, _ = one.shape
    return pl.pallas_call(
        finish_kernel,
        out_shape=jax.ShapeDtypeStruct((sessions, tokens, (size - 16) // tokens * HEAD), jnp.bfloat16),
        in_specs=[VMEM] * 3,
        out_specs=VMEM,
        compiler_params=pltpu.CompilerParams(vmem_limit_bytes=LIMIT),
    )(one, two, three)


def per_device(queries, cache_keys, stored_values, new_keys, new_values, lengths, positions):
    member = lax.axis_index("ctx")
    tokens = queries.shape[1]
    slots = cache_keys.shape[1]
    bases = jnp.stack([member, member ^ 1, member ^ 4, member ^ 5]) * slots
    scal = jnp.concatenate([lengths, bases]).astype(jnp.int32)

    near_q = pack_queries(queries, positions)
    near_x = [swap(near_q[s], 12) for s in range(near_q.shape[0])]
    far_q = swap(near_q, 2)
    own = pack_keys(positions, cache_keys, stored_values, new_keys, new_values)
    x_own = swap(own, 4)
    pair = swap(own, 1)
    far_q, scal, *near_x = lax.optimization_barrier((far_q, scal, *near_x))
    far_x = pass_on(swap(far_q, 12))
    x_own, far_q = lax.optimization_barrier((x_own, far_q))
    blocks = (own, pair, x_own, swap(x_own, 1))

    far_b = attend(scal, far_x, blocks)
    far_came = swap(far_b, 12)
    far_b, far_q = lax.optimization_barrier((far_b, far_q))
    far_a = attend(scal, far_q, blocks)
    far_came, far_a = lax.optimization_barrier((far_came, far_a))
    far = merge(far_a, far_came)
    back = swap(far, 2)

    far, near_q, *near_x = lax.optimization_barrier((far, near_q, *near_x))
    near_b = attend(scal, jnp.stack(near_x), blocks)
    near_came = swap(near_b, 12)
    near_b, near_q = lax.optimization_barrier((near_b, near_q))
    near_a = attend(scal, near_q, blocks)
    return finish(near_a, near_came, back, tokens)


def solution(mesh):
    spec = P("rep", "ctx", "tp")
    return jax.shard_map(
        per_device,
        mesh=mesh,
        in_specs=(spec, spec, spec, spec, spec, P("rep"), P("rep", "ctx")),
        out_specs=spec,
        check_vma=False,
    )
```

```python
import functools

import jax
import jax.numpy as jnp
from jax import lax
from jax.experimental import pallas as pl
from jax.experimental.pallas import tpu as pltpu
from jax.sharding import PartitionSpec as P

HEAD = 128
NEG = -1e30
VMEM = pl.BlockSpec(memory_space=pltpu.VMEM)
SMEM = pl.BlockSpec(memory_space=pltpu.SMEM)
LIMIT = 48 * 1024 * 1024
STEER = 16000000000
PACK = 48 * 1024 * 1024
SCALE = 1.0 / HEAD**0.5


def swap(block, mask):
    count = lax.axis_size("ctx")
    return lax.ppermute(block, "ctx", [(i, i ^ mask) for i in range(count)])


def column(row, rows, period):
    r = lax.broadcasted_iota(jnp.int32, (rows, 128), 0) % period
    c = lax.broadcasted_iota(jnp.int32, (rows, 128), 1)
    spread = jnp.broadcast_to(row, (rows, 128))
    return jnp.sum(jnp.where(r == c, spread, 0.0), axis=1, keepdims=True)


def lane_row(spread):
    r = lax.broadcasted_iota(jnp.int32, (128, 128), 0)
    c = lax.broadcasted_iota(jnp.int32, (128, 128), 1)
    return jnp.sum(jnp.where(r == c, jnp.broadcast_to(spread, (128, 128)), 0.0), axis=0, keepdims=True)


def stat_block(lse):
    halves = jnp.concatenate([lane_row(lse[:128]), lane_row(lse[128:])], axis=0)
    hi = halves.astype(jnp.bfloat16).astype(jnp.float32)
    rest = halves - hi
    mid = rest.astype(jnp.bfloat16).astype(jnp.float32)
    low = rest - mid
    blank = jnp.zeros((10, 128), jnp.float32)
    return jnp.concatenate([hi, mid, low, blank], axis=0).astype(jnp.bfloat16)


def read_stats(block):
    block = block.astype(jnp.float32)
    halves = block[0:2] + block[2:4] + block[4:6]
    return jnp.concatenate([column(halves[0:1], 128, 128), column(halves[1:2], 128, 128)], axis=0)


def place_block(row):
    shape = (16, row.shape[1])
    line = lax.broadcasted_iota(jnp.int32, shape, 0)
    spread = jnp.broadcast_to(row, shape)
    pieces = jnp.where(line == 0, spread >> 7, jnp.where(line == 1, spread & 127, 0))
    return pieces.astype(jnp.float32).astype(jnp.bfloat16)


def put_places(out, s, at, places):
    out[s, at : at + 16, :] = jnp.zeros((16, HEAD), jnp.bfloat16)
    out[s, at : at + 16, 0 : places.shape[1]] = place_block(places[s : s + 1, :])


def read_places(block):
    block = block.astype(jnp.float32)
    return block[0:1] * 128.0 + block[1:2]


def pack_queries_kernel(tokens, queries, places, out):
    sessions, size, _ = out.shape
    for s in range(sessions):
        for h in range((size - 16) // tokens):
            out[s, h * tokens : (h + 1) * tokens, :] = queries[s, :, h * HEAD : (h + 1) * HEAD]
        put_places(out, s, size - 16, places)


def pack_queries(queries, places):
    sessions, tokens, width = queries.shape
    return pl.pallas_call(
        functools.partial(pack_queries_kernel, tokens),
        out_shape=jax.ShapeDtypeStruct((sessions, width // HEAD * tokens + 16, HEAD), jnp.bfloat16),
        in_specs=[VMEM] * 2,
        out_specs=VMEM,
        compiler_params=pltpu.CompilerParams(vmem_limit_bytes=LIMIT),
    )(queries, places)


def pack_keys_kernel(slots, fresh, places, k, v, nk, nv, out, spots, sems):
    copies = [pltpu.make_async_copy(places, spots, sems.at[4])]
    at = 0
    for i, (ref, size) in enumerate(((k, slots), (v, slots), (nk, fresh), (nv, fresh))):
        copies.append(pltpu.make_async_copy(ref, out.at[:, pl.ds(at, size)], sems.at[i]))
        at += size
    for copy in copies:
        copy.start()
    copies[0].wait()
    for s in range(out.shape[0]):
        put_places(out, s, at, spots)
    for copy in copies[1:]:
        copy.wait()


def pack_keys(places, k, v, nk, nv):
    sessions, slots, _ = k.shape
    fresh = nk.shape[1]
    shape = (sessions, 2 * (slots + fresh) + 16, HEAD)
    return pl.pallas_call(
        functools.partial(pack_keys_kernel, slots, fresh),
        out_shape=pltpu.VMEM(shape, jnp.bfloat16),
        in_specs=[pl.BlockSpec(memory_space=pltpu.HBM)] * 5,
        out_specs=VMEM,
        scratch_shapes=[pltpu.VMEM(places.shape, places.dtype), pltpu.SemaphoreType.DMA((5,))],
        compiler_params=pltpu.CompilerParams(vmem_limit_bytes=PACK),
    )(*(pltpu.with_memory_space_constraint(x, pltpu.HBM) for x in (places, k, v, nk, nv)))


def attend_kernel(scal, q, s0, s1, s2, s3, out):
    blocks = (s0, s1, s2, s3)
    sessions, size, _ = q.shape
    rows = size - 16
    fresh = 128 // len(blocks)
    slots = (s0.shape[1] - 16) // 2 - fresh
    nk = 2 * slots
    cells = lax.broadcasted_iota(jnp.int32, (1, slots), 1)
    nt = (((1,), (1,)), ((), ()))
    left = [[scal[s] - scal[sessions + b] for b in range(len(blocks))] for s in range(sessions)]

    def score(s, b, masked):
        mine = q[s, 0:rows, :]
        if b < len(blocks):
            got = lax.dot_general(mine, blocks[b][s, 0:slots, :], nt, preferred_element_type=jnp.float32)
            return jnp.where(cells < left[s][b], got, NEG) if masked else got
        qpos = column(read_places(q[s, rows:size, :]), rows, fresh)
        kpos = [read_places(blk[s, nk + 2 * fresh : nk + 2 * fresh + 16, :])[:, 0:fresh] for blk in blocks]
        new_keys = jnp.concatenate([blk[s, nk : nk + fresh, :] for blk in blocks], axis=0)
        got = lax.dot_general(mine, new_keys, nt, preferred_element_type=jnp.float32)
        return jnp.where(jnp.concatenate(kpos, axis=1) <= qpos, got, NEG)

    def weigh(s, b, got, state):
        shift = jnp.max(got, axis=1, keepdims=True) * SCALE
        if state is not None:
            shift = jnp.maximum(shift, state[0])
        w = jnp.exp(got * SCALE - shift)
        total = functools.reduce(jnp.add, [w[:, j : j + 128] for j in range(0, w.shape[1], 128)])
        if b < len(blocks):
            v = blocks[b][s, slots:nk, :]
        else:
            v = jnp.concatenate([blk[s, nk + fresh : nk + 2 * fresh, :] for blk in blocks], axis=0)
        summed = jnp.dot(w.astype(jnp.bfloat16), v, preferred_element_type=jnp.float32)
        if state is not None:
            scale = jnp.exp(state[0] - shift)
            total += scale * state[1]
            summed += scale * state[2]
        return shift, total, summed

    def body(masked):
        units = [(s, b) for b in (len(blocks), *range(len(blocks))) for s in range(sessions)]
        states = [None] * sessions
        ahead = score(*units[0], masked)
        for n, (s, b) in enumerate(units):
            got = ahead
            if n + 1 < len(units):
                ahead = score(*units[n + 1], masked)
            states[s] = weigh(s, b, got, states[s])
        for s, (shift, total, summed) in enumerate(states):
            total = jnp.sum(total, axis=1, keepdims=True)
            out[s, 0:rows, :] = (summed / total).astype(jnp.bfloat16)
            out[s, rows:size, :] = stat_block(shift + jnp.log(total))

    full = functools.reduce(jnp.logical_and, [x >= slots for row in left for x in row])
    pl.when(full)(lambda: body(False))
    pl.when(jnp.logical_not(full))(lambda: body(True))


def attend(scal, q, blocks):
    return pl.pallas_call(
        attend_kernel,
        out_shape=jax.ShapeDtypeStruct(q.shape, jnp.bfloat16),
        in_specs=[SMEM] + [VMEM] * (1 + len(blocks)),
        out_specs=VMEM,
        compiler_params=pltpu.CompilerParams(vmem_limit_bytes=LIMIT),
        cost_estimate=pl.CostEstimate(flops=q.size, bytes_accessed=0, transcendentals=0),
    )(scal, q, *blocks)


def pass_on_kernel(came, out):
    out[...] = came[...]


def pass_on(came, cost):
    return pl.pallas_call(
        pass_on_kernel,
        out_shape=jax.ShapeDtypeStruct(came.shape, came.dtype),
        in_specs=[VMEM],
        out_specs=VMEM,
        compiler_params=pltpu.CompilerParams(vmem_limit_bytes=LIMIT),
        cost_estimate=pl.CostEstimate(flops=cost, bytes_accessed=0, transcendentals=0),
    )(came)


def merged(rows, messages):
    logs = [read_stats(m[rows : rows + 16, :]) for m in messages]
    top = functools.reduce(jnp.maximum, logs)
    shares = [jnp.exp(x - top) for x in logs]
    total = sum(shares)
    value = sum(m[:rows, :].astype(jnp.float32) * (x / total) for m, x in zip(messages, shares))
    return value, top + jnp.log(total)


def merge_kernel(own, came, out):
    sessions, size, _ = own.shape
    rows = size - 16
    for s in range(sessions):
        value, lse = merged(rows, [own[s], came[s]])
        out[s, 0:rows, :] = value.astype(jnp.bfloat16)
        out[s, rows:size, :] = stat_block(lse)


def merge(own, came):
    return pl.pallas_call(
        merge_kernel,
        out_shape=jax.ShapeDtypeStruct(own.shape, jnp.bfloat16),
        in_specs=[VMEM, VMEM],
        out_specs=VMEM,
        compiler_params=pltpu.CompilerParams(vmem_limit_bytes=LIMIT),
    )(own, came)


def finish_kernel(one, two, three, out):
    sessions, tokens, width = out.shape
    rows = one.shape[1] - 16
    for s in range(sessions):
        value, _ = merged(rows, [one[s], two[s], three[s]])
        value = value.astype(jnp.bfloat16)
        for h in range(width // HEAD):
            out[s, :, h * HEAD : (h + 1) * HEAD] = value[h * tokens : (h + 1) * tokens, :]


def finish(one, two, three, tokens):
    sessions, size, _ = one.shape
    return pl.pallas_call(
        finish_kernel,
        out_shape=jax.ShapeDtypeStruct((sessions, tokens, (size - 16) // tokens * HEAD), jnp.bfloat16),
        in_specs=[VMEM] * 3,
        out_specs=VMEM,
        compiler_params=pltpu.CompilerParams(vmem_limit_bytes=LIMIT),
    )(one, two, three)


def per_device(queries, cache_keys, stored_values, new_keys, new_values, lengths, positions):
    member = lax.axis_index("ctx")
    tokens = queries.shape[1]
    slots = cache_keys.shape[1]
    bases = jnp.stack([member, member ^ 1, member ^ 4, member ^ 5]) * slots
    scal = jnp.concatenate([lengths, bases]).astype(jnp.int32)

    near_q = pack_queries(queries, positions)
    near_x = [swap(near_q[s], 12) for s in range(near_q.shape[0])]
    far_q = swap(near_q, 2)
    own = pack_keys(positions, cache_keys, stored_values, new_keys, new_values)
    x_own = swap(own, 4)
    pair = swap(own, 1)
    far_q, scal, *near_x = lax.optimization_barrier((far_q, scal, *near_x))
    far_x = pass_on(swap(far_q, 12), STEER)
    x_own, far_q = lax.optimization_barrier((x_own, far_q))
    blocks = (own, pair, x_own, swap(x_own, 1))

    far_b = attend(scal, far_x, blocks)
    far_came = swap(far_b, 12)
    far_b, far_q = lax.optimization_barrier((far_b, far_q))
    far_a = attend(scal, far_q, blocks)
    far_came, far_a = lax.optimization_barrier((far_came, far_a))
    far = merge(far_a, far_came)
    back = pass_on(swap(far, 2), 10**9)

    far, near_q, *near_x = lax.optimization_barrier((far, near_q, *near_x))
    near_b = attend(scal, jnp.stack(near_x), blocks)
    near_came = swap(near_b, 12)
    near_b, near_q = lax.optimization_barrier((near_b, near_q))
    near_a = attend(scal, near_q, blocks)
    return finish(near_a, near_came, back, tokens)


def solution(mesh):
    spec = P("rep", "ctx", "tp")
    return jax.shard_map(
        per_device,
        mesh=mesh,
        in_specs=(spec, spec, spec, spec, spec, P("rep"), P("rep", "ctx")),
        out_specs=spec,
        check_vma=False,
    )
```

```python
import functools

import jax
import jax.numpy as jnp
from jax import lax
from jax.experimental import pallas as pl
from jax.experimental.pallas import tpu as pltpu
from jax.sharding import PartitionSpec as P

HEAD = 128
NEG = -1e30
VMEM = pl.BlockSpec(memory_space=pltpu.VMEM)
SMEM = pl.BlockSpec(memory_space=pltpu.SMEM)
LIMIT = 48 * 1024 * 1024
STEER = 16000000000
PACK = 48 * 1024 * 1024
SCALE = 1.0 / HEAD**0.5


def swap(block, mask):
    count = lax.axis_size("ctx")
    return lax.ppermute(block, "ctx", [(i, i ^ mask) for i in range(count)])


def column(row, rows, period):
    r = lax.broadcasted_iota(jnp.int32, (rows, 128), 0) % period
    c = lax.broadcasted_iota(jnp.int32, (rows, 128), 1)
    spread = jnp.broadcast_to(row, (rows, 128))
    return jnp.sum(jnp.where(r == c, spread, 0.0), axis=1, keepdims=True)


def lane_row(spread):
    r = lax.broadcasted_iota(jnp.int32, (128, 128), 0)
    c = lax.broadcasted_iota(jnp.int32, (128, 128), 1)
    return jnp.sum(jnp.where(r == c, jnp.broadcast_to(spread, (128, 128)), 0.0), axis=0, keepdims=True)


def stat_block(lse):
    halves = jnp.concatenate([lane_row(lse[:128]), lane_row(lse[128:])], axis=0)
    hi = halves.astype(jnp.bfloat16).astype(jnp.float32)
    rest = halves - hi
    mid = rest.astype(jnp.bfloat16).astype(jnp.float32)
    low = rest - mid
    blank = jnp.zeros((10, 128), jnp.float32)
    return jnp.concatenate([hi, mid, low, blank], axis=0).astype(jnp.bfloat16)


def read_stats(block):
    block = block.astype(jnp.float32)
    halves = block[0:2] + block[2:4] + block[4:6]
    return jnp.concatenate([column(halves[0:1], 128, 128), column(halves[1:2], 128, 128)], axis=0)


def place_block(row):
    shape = (16, row.shape[1])
    line = lax.broadcasted_iota(jnp.int32, shape, 0)
    spread = jnp.broadcast_to(row, shape)
    pieces = jnp.where(line == 0, spread >> 7, jnp.where(line == 1, spread & 127, 0))
    return pieces.astype(jnp.float32).astype(jnp.bfloat16)


def put_places(out, s, at, places):
    out[s, at : at + 16, :] = jnp.zeros((16, HEAD), jnp.bfloat16)
    out[s, at : at + 16, 0 : places.shape[1]] = place_block(places[s : s + 1, :])


def read_places(block):
    block = block.astype(jnp.float32)
    return block[0:1] * 128.0 + block[1:2]


def pack_queries_kernel(tokens, queries, places, out):
    sessions, size, _ = out.shape
    for s in range(sessions):
        for h in range((size - 16) // tokens):
            out[s, h * tokens : (h + 1) * tokens, :] = queries[s, :, h * HEAD : (h + 1) * HEAD]
        put_places(out, s, size - 16, places)


def pack_queries(queries, places):
    sessions, tokens, width = queries.shape
    return pl.pallas_call(
        functools.partial(pack_queries_kernel, tokens),
        out_shape=jax.ShapeDtypeStruct((sessions, width // HEAD * tokens + 16, HEAD), jnp.bfloat16),
        in_specs=[VMEM] * 2,
        out_specs=VMEM,
        compiler_params=pltpu.CompilerParams(vmem_limit_bytes=LIMIT),
    )(queries, places)


def pack_keys_kernel(slots, fresh, places, k, v, nk, nv, out, spots, sems):
    copies = [pltpu.make_async_copy(places, spots, sems.at[4])]
    at = 0
    for i, (ref, size) in enumerate(((k, slots), (v, slots), (nk, fresh), (nv, fresh))):
        copies.append(pltpu.make_async_copy(ref, out.at[:, pl.ds(at, size)], sems.at[i]))
        at += size
    for copy in copies:
        copy.start()
    copies[0].wait()
    for s in range(out.shape[0]):
        put_places(out, s, at, spots)
    for copy in copies[1:]:
        copy.wait()


def pack_keys(places, k, v, nk, nv):
    sessions, slots, _ = k.shape
    fresh = nk.shape[1]
    shape = (sessions, 2 * (slots + fresh) + 16, HEAD)
    return pl.pallas_call(
        functools.partial(pack_keys_kernel, slots, fresh),
        out_shape=pltpu.VMEM(shape, jnp.bfloat16),
        in_specs=[pl.BlockSpec(memory_space=pltpu.HBM)] * 5,
        out_specs=VMEM,
        scratch_shapes=[pltpu.VMEM(places.shape, places.dtype), pltpu.SemaphoreType.DMA((5,))],
        compiler_params=pltpu.CompilerParams(vmem_limit_bytes=PACK),
    )(*(pltpu.with_memory_space_constraint(x, pltpu.HBM) for x in (places, k, v, nk, nv)))


def attend_kernel(scal, q, s0, s1, s2, s3, out):
    blocks = (s0, s1, s2, s3)
    sessions, size, _ = q.shape
    rows = size - 16
    fresh = 128 // len(blocks)
    slots = (s0.shape[1] - 16) // 2 - fresh
    nk = 2 * slots
    cells = lax.broadcasted_iota(jnp.int32, (1, slots), 1)
    nt = (((1,), (1,)), ((), ()))
    left = [[scal[s] - scal[sessions + b] for b in range(len(blocks))] for s in range(sessions)]

    def score(s, b, masked):
        mine = q[s, 0:rows, :]
        if b < len(blocks):
            got = lax.dot_general(mine, blocks[b][s, 0:slots, :], nt, preferred_element_type=jnp.float32)
            return jnp.where(cells < left[s][b], got, NEG) if masked else got
        qpos = column(read_places(q[s, rows:size, :]), rows, fresh)
        kpos = [read_places(blk[s, nk + 2 * fresh : nk + 2 * fresh + 16, :])[:, 0:fresh] for blk in blocks]
        new_keys = jnp.concatenate([blk[s, nk : nk + fresh, :] for blk in blocks], axis=0)
        got = lax.dot_general(mine, new_keys, nt, preferred_element_type=jnp.float32)
        return jnp.where(jnp.concatenate(kpos, axis=1) <= qpos, got, NEG)

    def weigh(s, b, got, state):
        shift = jnp.max(got, axis=1, keepdims=True) * SCALE
        if state is not None:
            shift = jnp.maximum(shift, state[0])
        w = jnp.exp(got * SCALE - shift)
        total = functools.reduce(jnp.add, [w[:, j : j + 128] for j in range(0, w.shape[1], 128)])
        if b < len(blocks):
            v = blocks[b][s, slots:nk, :]
        else:
            v = jnp.concatenate([blk[s, nk + fresh : nk + 2 * fresh, :] for blk in blocks], axis=0)
        summed = jnp.dot(w.astype(jnp.bfloat16), v, preferred_element_type=jnp.float32)
        if state is not None:
            scale = jnp.exp(state[0] - shift)
            total += scale * state[1]
            summed += scale * state[2]
        return shift, total, summed

    def body(masked):
        units = [(s, b) for b in (len(blocks), *range(len(blocks))) for s in range(sessions)]
        states = [None] * sessions
        ahead = [score(*u, masked) for u in units[:2]]
        for n, (s, b) in enumerate(units):
            got = ahead.pop(0)
            if n + 2 < len(units):
                ahead.append(score(*units[n + 2], masked))
            states[s] = weigh(s, b, got, states[s])
        for s, (shift, total, summed) in enumerate(states):
            total = jnp.sum(total, axis=1, keepdims=True)
            out[s, 0:rows, :] = (summed / total).astype(jnp.bfloat16)
            out[s, rows:size, :] = stat_block(shift + jnp.log(total))

    full = functools.reduce(jnp.logical_and, [x >= slots for row in left for x in row])
    pl.when(full)(lambda: body(False))
    pl.when(jnp.logical_not(full))(lambda: body(True))


def attend(scal, q, blocks):
    return pl.pallas_call(
        attend_kernel,
        out_shape=jax.ShapeDtypeStruct(q.shape, jnp.bfloat16),
        in_specs=[SMEM] + [VMEM] * (1 + len(blocks)),
        out_specs=VMEM,
        compiler_params=pltpu.CompilerParams(vmem_limit_bytes=LIMIT),
        cost_estimate=pl.CostEstimate(flops=q.size, bytes_accessed=0, transcendentals=0),
    )(scal, q, *blocks)


def pass_on_kernel(came, out):
    out[...] = came[...]


def pass_on(came, cost):
    return pl.pallas_call(
        pass_on_kernel,
        out_shape=jax.ShapeDtypeStruct(came.shape, came.dtype),
        in_specs=[VMEM],
        out_specs=VMEM,
        compiler_params=pltpu.CompilerParams(vmem_limit_bytes=LIMIT),
        cost_estimate=pl.CostEstimate(flops=cost, bytes_accessed=0, transcendentals=0),
    )(came)


def merged(rows, messages):
    logs = [read_stats(m[rows : rows + 16, :]) for m in messages]
    top = functools.reduce(jnp.maximum, logs)
    shares = [jnp.exp(x - top) for x in logs]
    total = sum(shares)
    value = sum(m[:rows, :].astype(jnp.float32) * (x / total) for m, x in zip(messages, shares))
    return value, top + jnp.log(total)


def merge_kernel(own, came, out):
    sessions, size, _ = own.shape
    rows = size - 16
    for s in range(sessions):
        value, lse = merged(rows, [own[s], came[s]])
        out[s, 0:rows, :] = value.astype(jnp.bfloat16)
        out[s, rows:size, :] = stat_block(lse)


def merge(own, came):
    return pl.pallas_call(
        merge_kernel,
        out_shape=jax.ShapeDtypeStruct(own.shape, jnp.bfloat16),
        in_specs=[VMEM, VMEM],
        out_specs=VMEM,
        compiler_params=pltpu.CompilerParams(vmem_limit_bytes=LIMIT),
    )(own, came)


def finish_kernel(one, two, three, out):
    sessions, tokens, width = out.shape
    rows = one.shape[1] - 16
    for s in range(sessions):
        value, _ = merged(rows, [one[s], two[s], three[s]])
        value = value.astype(jnp.bfloat16)
        for h in range(width // HEAD):
            out[s, :, h * HEAD : (h + 1) * HEAD] = value[h * tokens : (h + 1) * tokens, :]


def finish(one, two, three, tokens):
    sessions, size, _ = one.shape
    return pl.pallas_call(
        finish_kernel,
        out_shape=jax.ShapeDtypeStruct((sessions, tokens, (size - 16) // tokens * HEAD), jnp.bfloat16),
        in_specs=[VMEM] * 3,
        out_specs=VMEM,
        compiler_params=pltpu.CompilerParams(vmem_limit_bytes=LIMIT),
    )(one, two, three)


def per_device(queries, cache_keys, stored_values, new_keys, new_values, lengths, positions):
    member = lax.axis_index("ctx")
    tokens = queries.shape[1]
    slots = cache_keys.shape[1]
    bases = jnp.stack([member, member ^ 1, member ^ 4, member ^ 5]) * slots
    scal = jnp.concatenate([lengths, bases]).astype(jnp.int32)

    near_q = pack_queries(queries, positions)
    near_x = [swap(near_q[s], 12) for s in range(near_q.shape[0])]
    far_q = swap(near_q, 2)
    own = pack_keys(positions, cache_keys, stored_values, new_keys, new_values)
    x_own = swap(own, 4)
    pair = swap(own, 1)
    far_q, scal, *near_x = lax.optimization_barrier((far_q, scal, *near_x))
    far_x = pass_on(swap(far_q, 12), STEER)
    x_own, far_q = lax.optimization_barrier((x_own, far_q))
    blocks = (own, pair, x_own, swap(x_own, 1))

    far_b = attend(scal, far_x, blocks)
    far_came = swap(far_b, 12)
    far_b, far_q = lax.optimization_barrier((far_b, far_q))
    far_a = attend(scal, far_q, blocks)
    far_came, far_a = lax.optimization_barrier((far_came, far_a))
    far = merge(far_a, far_came)
    back = pass_on(swap(far, 2), 10**9)

    far, near_q, *near_x = lax.optimization_barrier((far, near_q, *near_x))
    near_b = attend(scal, jnp.stack(near_x), blocks)
    near_came = swap(near_b, 12)
    near_b, near_q = lax.optimization_barrier((near_b, near_q))
    near_a = attend(scal, near_q, blocks)
    return finish(near_a, near_came, back, tokens)


def solution(mesh):
    spec = P("rep", "ctx", "tp")
    return jax.shard_map(
        per_device,
        mesh=mesh,
        in_specs=(spec, spec, spec, spec, spec, P("rep"), P("rep", "ctx")),
        out_specs=spec,
        check_vma=False,
    )
```
